256 devices in a mesh: pitch: 16 (over x_hi, z), inst: 8 (over y, core), span: 2 (over x_lo).
Axes of the slice: x: 4 (x_hi: 2, x_lo: 2; x = x_hi * 2 + x_lo), y: 4, z: 8, core: 2. Of those that a mesh axis runs over, the one named last changes fastest.
Arguments:
- donor_state: float32 [2, 24, 5, 128, 2048], P(None, 'inst', None, 'span', 'pitch'), may hold values from -6 to 6
- time_shift: float32 [2, 17, 17], replicated, may hold values from -1.5 to 1.5
- face_shift: int32 [17], replicated, may hold values from 0 to 1023, as said below
- weights: float32 [2, 4, 2048], P(None, None, 'pitch'), may hold values from 0.1 to 0.5
- offsets: int32 [2, 4], replicated, may hold values from -3 to 3
Outputs:
- received: float32 [2, 24, 5, 128, 2048], P(None, 'inst', None, 'span', 'pitch')
The draws below stay inside these ranges and needn't reach their ends.
Inputs may be any that keep to these rules, and one draw needn't show every extreme that they name: `face_shift`: at least one instance has a shift of 960 or more.
All inputs are finite; a program needn't handle non-finite values.
Results may differ from the reference program's by a relative error of at most 0.00007.
Values sent between devices are 32-bit elements; how exact they have to be, the bound alone decides.
No kernel may reach another device: no remote copies, remote signals or barrier semaphores. Data moves between devices by JAX's collectives and lax.ppermute only.
A program may use at most 128 MiB of HBM per device.

```python
import math
import jax
import jax.numpy as jnp
from jax import lax

INSTANCES = 17
VARS = 5
BAND = 4
HALO = 3
PITCH_DEV = 128
REACH = 8
INST_PAD = 24
PITCH = 2048
SPAN = 128


def draw_face_shift(key, part):
    limit = REACH * PITCH_DEV
    base = jax.random.randint(jax.random.fold_in(key, 11), (INSTANCES,), 0, limit, dtype=jnp.int32)
    chosen = jax.random.randint(jax.random.fold_in(key, 12), (), 0, INSTANCES, dtype=jnp.int32)
    high = limit - 1 - jax.random.randint(jax.random.fold_in(key, 13), (), 0, PITCH_DEV // 2, dtype=jnp.int32)
    places = jnp.arange(INSTANCES, dtype=jnp.int32)
    return jnp.where(places == chosen, high, base).astype(jnp.int32)


def place_ends(entries, stream_key, smallest, high):
    place = [jax.random.randint(jax.random.fold_in(stream_key, axis), (), 0, length) for axis, length in enumerate(entries.shape)]
    widest = entries.shape.index(max(entries.shape))
    next_to = place[:widest] + [(place[widest] + 1) % entries.shape[widest]] + place[widest + 1:]
    return entries.at[tuple(place)].set(smallest).at[tuple(next_to)].set(high)


def block_scale(key, dims, shards, low, high):
    def one(position, blocks):
        draws = jax.random.uniform(jax.random.fold_in(jax.random.fold_in(key, 6), position), (blocks,), jnp.float32, low / len(shards), high / len(shards))
        return jnp.repeat(jnp.exp(draws), dims[position] // blocks).reshape((-1,) + (1,) * (len(dims) - position - 1))

    gain = one(*shards[0])
    for cut in shards[1:]:
        gain = gain * one(*cut)
    return gain


def centred(own_key, extent, deviation, reach, cuts=(), held_as=jnp.bfloat16):
    gain = block_scale(own_key, extent, cuts, -0.22, 0.18) if cuts else 1.0
    values = jax.random.normal(own_key, extent, jnp.float32) * deviation * gain
    return jnp.minimum(jnp.maximum(values, -reach), reach).astype(held_as)


def setup_inputs(seed: int = 0) -> dict:
    seeds = jax.random.split(jax.random.key(seed), 6)
    donor_state = centred(seeds[0], (2, INST_PAD, VARS, SPAN, PITCH), 1.0, 6.0, ((1, 8), (3, 2), (4, 16)), jnp.float32)
    time_shift = centred(seeds[1], (2, INSTANCES, INSTANCES), 0.25, 1.5, (), jnp.float32)
    face_shift = draw_face_shift(jax.random.fold_in(seeds[5], 71), 0)
    weights = jnp.clip(jnp.exp(math.log(0.5) - 1.609438 * jax.random.uniform(seeds[3], (2, BAND, PITCH), jnp.float32) ** block_scale(seeds[3], (2, BAND, PITCH), ((2, 16),), -0.2, 0.2)), 0.1, 0.5)
    offsets = place_ends(jax.random.randint(seeds[4], (2, BAND), 0 - HALO, HALO + 1), jax.random.fold_in(seeds[4], 1), 0 - HALO, HALO).astype(jnp.int32)
    return {"donor_state": donor_state, "time_shift": time_shift, "face_shift": face_shift, "weights": weights, "offsets": offsets}


def roll_one(field, amount):
    return jnp.roll(field, -amount, axis=-1)


def reference(donor_state, time_shift, face_shift, weights, offsets):
    donor = donor_state[:, :INSTANCES][::-1]
    resampled = jnp.einsum("rmk,rkvsp->rmvsp", time_shift, donor, precision=lax.Precision.HIGHEST)
    result = []
    for row in range(2):
        sign = 1 - 2 * row
        summed = jnp.zeros(resampled.shape[1:], jnp.float32)
        for member in range(BAND):
            amounts = (sign * face_shift + offsets[row, member]).astype(jnp.int32)
            moved = jax.vmap(roll_one)(resampled[row], amounts)
            summed = summed + weights[row, member][None, None, None, :] * moved
        result.append(summed)
    stacked = jnp.stack(result)
    filler = jnp.zeros((2, INST_PAD - INSTANCES) + stacked.shape[2:], jnp.float32)
    return jnp.concatenate([stacked, filler], axis=1)
```

```python
import functools

import jax
import jax.numpy as jnp
from jax import lax
from jax.experimental import pallas as pl
from jax.experimental.pallas import tpu as pltpu
from jax.sharding import PartitionSpec as P

VARS = 5
ROWS = 16
VMEM = pl.BlockSpec(memory_space=pltpu.VMEM)
SMEM = pl.BlockSpec(memory_space=pltpu.SMEM)


def pack_kernel(donor_ref, weights_ref, sent_ref):
    inst_dev, span = donor_ref.shape[1], donor_ref.shape[3]
    members = weights_ref.shape[1]
    member = lax.rem(lax.axis_index("inst"), members)
    for r in range(2):
        first = r * span * ROWS
        for k in range(inst_dev):
            for v in range(VARS):
                sent_ref[pl.ds(first + k * VARS + v, span, stride=ROWS), :] = donor_ref[1 - r, k, v]
        row = weights_ref[r, pl.ds(member, 1), :]
        sent_ref[pl.ds(first + ROWS - 1, span, stride=ROWS), :] = jnp.broadcast_to(row, (span, row.shape[1]))


def mixing_matrix(matrix, inst_dev, rows, cols):
    count = matrix.shape[0]
    high = lax.Precision.HIGHEST
    row_id = lax.broadcasted_iota(jnp.int32, (rows, count), 0)
    pick_row = (row_id // 8 == lax.broadcasted_iota(jnp.int32, (rows, count), 1)).astype(jnp.float32)
    col_id = lax.broadcasted_iota(jnp.int32, (count, cols), 1)
    source = (col_id // ROWS) * inst_dev + lax.rem(col_id, ROWS) // VARS
    pick_col = (source == lax.broadcasted_iota(jnp.int32, (count, cols), 0)).astype(jnp.float32)
    spread = jnp.dot(
        pick_row,
        jnp.dot(matrix, pick_col, precision=high, preferred_element_type=jnp.float32),
        precision=high,
        preferred_element_type=jnp.float32,
    )
    row_id = lax.broadcasted_iota(jnp.int32, (rows, cols), 0)
    col_id = lax.rem(lax.broadcasted_iota(jnp.int32, (rows, cols), 1), ROWS)
    row_var = lax.rem(lax.rem(row_id, 8) + 8 * VARS - VARS * lax.rem(row_id // 8, inst_dev), 8)
    keep = (row_var == lax.rem(col_id, VARS)) & (col_id < inst_dev * VARS)
    return jnp.where(keep, spread, 0.0)


def transfer_kernel(
    inst_dev, blocks, got_ref, time_shift_ref, face_shift_ref, offsets_ref, sent_ref, mixed_ref, weight_ref
):
    members = offsets_ref.shape[1]
    count = time_shift_ref.shape[1]
    lanes = got_ref.shape[1]
    depth = got_ref.shape[0] // blocks
    owners = depth // ROWS
    position = lax.axis_index("pitch") * owners + lax.axis_index("inst")
    row = position // (blocks * owners // 2)
    sign = 1 - 2 * row
    mix = mixing_matrix(time_shift_ref[row], inst_dev, count * 8, depth)
    for block in range(blocks):
        part = jnp.dot(
            mix,
            got_ref[block * depth : (block + 1) * depth, :],
            precision=lax.Precision.HIGHEST,
            preferred_element_type=jnp.float32,
        )
        mixed_ref[block] = part
        mixed_ref[block + blocks] = part
        for member in range(members):
            at = block * depth + member * ROWS + ROWS - 1
            weight_ref[member, block] = jnp.broadcast_to(got_ref[at : at + 1, :], (8, lanes))
    lane = lax.broadcasted_iota(jnp.int32, (1, 1, lanes), 2)
    sub = lax.broadcasted_iota(jnp.int32, (1, 8, 1), 1)

    def interpolated(m):
        total = jnp.zeros((blocks, 8, lanes), jnp.float32)
        for member in range(members):
            start = sign * face_shift_ref[m] + offsets_ref[row, member] + blocks * lanes
            start = lax.rem(start, blocks * lanes)
            skip, turn = start // lanes, lax.rem(start, lanes)
            window = mixed_ref[pl.ds(skip, blocks + 1), m * 8 : (m + 1) * 8, :]
            turned = pltpu.roll(window.reshape((blocks + 1) * 8, lanes), lax.rem(lanes - turn, lanes), 1)
            turned = turned.reshape(blocks + 1, 8, lanes)
            moved = jnp.where(lane < lanes - turn, turned[:blocks], turned[1:])
            total = total + weight_ref[member] * moved
        return total

    zero = jnp.zeros((blocks, 8, lanes), jnp.float32)
    for owner in range(owners):
        parts = [interpolated(m) if m < count else zero for m in range(owner * inst_dev, (owner + 1) * inst_dev)]
        low = jnp.where(sub < VARS, parts[0], parts[1])
        high = jnp.where(sub < 2 * VARS - 8, parts[1], parts[2])
        sent_ref[:, owner * ROWS : owner * ROWS + 8, :] = low
        sent_ref[:, owner * ROWS + 8 : (owner + 1) * ROWS, :] = high


def unpack_kernel(got_ref, received_ref):
    inst_dev, span = received_ref.shape[1], received_ref.shape[3]
    for r in range(2):
        for k in range(inst_dev):
            for v in range(VARS):
                at = r * span * ROWS + k * VARS + v
                received_ref[r, k, v] = got_ref[pl.ds(at, span, stride=ROWS), :]


def on_device(donor_state, time_shift, face_shift, weights, offsets):
    inst_dev, lanes = donor_state.shape[1], donor_state.shape[4]
    blocks, owners = lax.axis_size("pitch"), lax.axis_size("inst")
    peers = blocks * owners
    members = weights.shape[1]
    flat = jax.ShapeDtypeStruct((peers * ROWS, lanes), jnp.float32)

    def exchanged(x):
        whole = x.reshape(peers, ROWS, lanes)
        return lax.all_to_all(whole, ("pitch", "inst"), 0, 0, tiled=True).reshape(flat.shape)

    packed = pl.pallas_call(pack_kernel, out_shape=flat, in_specs=[VMEM, VMEM], out_specs=VMEM)(donor_state, weights)
    got = exchanged(packed)
    sent = pl.pallas_call(
        functools.partial(transfer_kernel, inst_dev, blocks),
        out_shape=jax.ShapeDtypeStruct((blocks, owners * ROWS, lanes), jnp.float32),
        in_specs=[VMEM, VMEM, SMEM, SMEM],
        out_specs=VMEM,
        scratch_shapes=[
            pltpu.VMEM((2 * blocks, time_shift.shape[1] * 8, lanes), jnp.float32),
            pltpu.VMEM((members, blocks, 8, lanes), jnp.float32),
        ],
        compiler_params=pltpu.CompilerParams(vmem_limit_bytes=24 * 2**20),
    )(got, time_shift, face_shift, offsets)
    back = exchanged(sent)
    return pl.pallas_call(
        unpack_kernel,
        out_shape=jax.ShapeDtypeStruct(donor_state.shape, jnp.float32),
        in_specs=[VMEM],
        out_specs=VMEM,
    )(back)


def solution(mesh):
    return jax.shard_map(
        on_device,
        mesh=mesh,
        in_specs=(P(None, "inst", None, "span", "pitch"), P(), P(), P(None, None, "pitch"), P()),
        out_specs=P(None, "inst", None, "span", "pitch"),
        check_vma=False,
    )
```

```python
import functools

import jax
import jax.numpy as jnp
from jax import lax
from jax.experimental import pallas as pl
from jax.experimental.pallas import tpu as pltpu
from jax.sharding import PartitionSpec as P

VARS = 5
SUB = 8
VMEM = pl.BlockSpec(memory_space=pltpu.VMEM)
SMEM = pl.BlockSpec(memory_space=pltpu.SMEM)


def params(mib):
    return pltpu.CompilerParams(vmem_limit_bytes=mib * 2**20)


def ceil_to(value, unit):
    return -(-value // unit) * unit


def mixing_matrix(matrix, inst_dev, rows, cols):
    count = matrix.shape[0]
    high = lax.Precision.HIGHEST
    row_id = lax.broadcasted_iota(jnp.int32, (rows, count), 0)
    pick_row = (row_id // SUB == lax.broadcasted_iota(jnp.int32, (rows, count), 1)).astype(jnp.float32)
    col_id = lax.broadcasted_iota(jnp.int32, (count, cols), 1)
    pick_col = (col_id // VARS == lax.broadcasted_iota(jnp.int32, (count, cols), 0)).astype(jnp.float32)
    spread = jnp.dot(
        pick_row,
        jnp.dot(matrix, pick_col, precision=high, preferred_element_type=jnp.float32),
        precision=high,
        preferred_element_type=jnp.float32,
    )
    row_id = lax.broadcasted_iota(jnp.int32, (rows, cols), 0)
    col_var = lax.rem(lax.broadcasted_iota(jnp.int32, (rows, cols), 1), VARS)
    row_var = lax.rem(lax.rem(row_id, SUB) + VARS * SUB * count - VARS * (row_id // SUB), SUB)
    return jnp.where(row_var == col_var, spread, 0.0)


def pack_kernel(half, donor_ref, weights_ref, time_shift_ref, sent_ref, mix_ref):
    inst_dev, span = donor_ref.shape[1], donor_ref.shape[3]
    count = time_shift_ref.shape[1]
    depth = inst_dev * VARS
    row = pl.program_id(0)
    for k in range(inst_dev):
        for v in range(VARS):
            sent_ref[pl.ds(k * VARS + v, span, stride=depth), :] = donor_ref[0, k, v]
    spare = -(-count // inst_dev)

    @pl.when(lax.axis_index("inst") == spare)
    def _():
        for member in range(weights_ref.shape[1]):
            one = weights_ref[row, member : member + 1, :]
            sent_ref[pl.ds(member, span, stride=depth), :] = jnp.broadcast_to(one, (span, one.shape[1]))

    @pl.when(row == 0)
    def _():
        mix_ref[...] = mixing_matrix(time_shift_ref[half()], inst_dev, *mix_ref.shape)


def split(x):
    high = x.astype(jnp.bfloat16)
    return high, (x - high.astype(jnp.float32)).astype(jnp.bfloat16)


def transfer_kernel(half, inst_dev, blocks, got_ref, mix_ref, face_shift_ref, offsets_ref, sent_ref, mixed_ref, weight_ref):
    members = offsets_ref.shape[1]
    count = face_shift_ref.shape[0]
    lanes = got_ref.shape[1]
    depth = got_ref.shape[0] // blocks
    period = blocks * lanes
    spare = -(-count // inst_dev) * inst_dev * VARS
    row = half()
    sign = 1 - 2 * row
    used = mix_ref.shape[1]
    mix_high, mix_low = split(mix_ref[...])
    mix = jnp.concatenate([mix_high, mix_high, mix_low], axis=1)
    for block in range(blocks):
        high, low = split(got_ref[block * depth : block * depth + used, :])
        part = jnp.dot(mix, jnp.concatenate([high, low, high], axis=0), preferred_element_type=jnp.float32)
        mixed_ref[block] = part
        mixed_ref[block + blocks] = part
        for member in range(members):
            at = block * depth + spare + member
            weight_ref[member, block] = jnp.broadcast_to(got_ref[at : at + 1, :], (SUB, lanes))
    lane = lax.broadcasted_iota(jnp.int32, (1, 1, lanes), 2)
    sub = lax.broadcasted_iota(jnp.int32, (1, SUB, 1), 1)

    def interpolated(m):
        total = None
        for member in range(members):
            start = lax.rem(sign * face_shift_ref[m] + offsets_ref[row, member] + period, period)
            skip, turn = start // lanes, lax.rem(start, lanes)
            window = mixed_ref[pl.ds(skip, blocks + 1), m * SUB : (m + 1) * SUB, :]
            turned = pltpu.roll(window.reshape((blocks + 1) * SUB, lanes), lax.rem(lanes - turn, lanes), 1)
            turned = turned.reshape(blocks + 1, SUB, lanes)
            term = weight_ref[member] * jnp.where(lane < lanes - turn, turned[:blocks], turned[1:])
            total = term if total is None else total + term
        return total

    parts = {}
    for tile in range(depth // SUB):
        first, last = tile * SUB // VARS, (tile * SUB + SUB - 1) // VARS
        joined = None
        for m in range(first, last + 1):
            if m >= count:
                part = jnp.zeros((blocks, SUB, lanes), jnp.float32)
            else:
                if m not in parts:
                    parts = {m - 1: parts[m - 1], m: interpolated(m)} if m - 1 in parts else {m: interpolated(m)}
                part = parts[m]
            joined = part if joined is None else jnp.where(sub >= m * VARS - tile * SUB, part, joined)
        sent_ref[:, tile * SUB : (tile + 1) * SUB, :] = joined


def unpack_kernel(got_ref, received_ref):
    inst_dev, span = received_ref.shape[1], received_ref.shape[3]
    depth = inst_dev * VARS
    first = pl.program_id(0) * span * depth
    for k in range(inst_dev):
        for v in range(VARS):
            received_ref[0, k, v] = got_ref[pl.ds(first + k * VARS + v, span, stride=depth), :]


def my_row(peers, owners):
    return (lax.axis_index("pitch") * owners + lax.axis_index("inst")) // (peers // 2)


def on_device(donor_state, time_shift, face_shift, weights, offsets, blocks=None, owners=None, exchange=None):
    _, inst_dev, _, span, lanes = donor_state.shape
    blocks, owners = blocks or lax.axis_size("pitch"), owners or lax.axis_size("inst")
    peers = blocks * owners
    members, count = weights.shape[1], time_shift.shape[1]
    depth = inst_dev * VARS
    used = ceil_to(count * VARS, SUB)
    half = functools.partial(my_row, peers, owners)

    def exchanged(x):
        whole = x.reshape(peers, depth, 1, lanes)
        return lax.all_to_all(whole, ("pitch", "inst"), 0, 0, tiled=True).reshape(peers * depth, lanes)

    exchanged = exchange or exchanged

    packed, mix = pl.pallas_call(
        functools.partial(pack_kernel, half),
        grid=(2,),
        out_shape=(
            jax.ShapeDtypeStruct((peers * depth, lanes), jnp.float32),
            jax.ShapeDtypeStruct((count * SUB, used), jnp.float32),
        ),
        in_specs=[
            pl.BlockSpec((1, inst_dev, VARS, span, lanes), lambda r: (1 - r, 0, 0, 0, 0)),
            VMEM,
            VMEM,
        ],
        out_specs=(pl.BlockSpec((span * depth, lanes), lambda r: (r, 0)), VMEM),
        compiler_params=params(8),
    )(donor_state, weights, time_shift)
    got = exchanged(packed)
    sent = pl.pallas_call(
        functools.partial(transfer_kernel, half, inst_dev, blocks),
        out_shape=jax.ShapeDtypeStruct((blocks, owners * depth, lanes), jnp.float32),
        in_specs=[VMEM, VMEM, SMEM, SMEM],
        out_specs=VMEM,
        scratch_shapes=[
            pltpu.VMEM((2 * blocks, count * SUB, lanes), jnp.float32),
            pltpu.VMEM((members, blocks, SUB, lanes), jnp.float32),
        ],
        compiler_params=params(24),
    )(got, mix, face_shift, offsets)
    back = exchanged(sent)
    return pl.pallas_call(
        unpack_kernel,
        grid=(2,),
        out_shape=jax.ShapeDtypeStruct(donor_state.shape, jnp.float32),
        in_specs=[VMEM],
        out_specs=pl.BlockSpec((1, inst_dev, VARS, span, lanes), lambda r: (r, 0, 0, 0, 0)),
        compiler_params=params(8),
    )(back)


def solution(mesh):
    return jax.shard_map(
        on_device,
        mesh=mesh,
        in_specs=(P(None, "inst", None, "span", "pitch"), P(), P(), P(None, None, "pitch"), P()),
        out_specs=P(None, "inst", None, "span", "pitch"),
        check_vma=False,
    )
```

```python
import functools

import jax
import jax.numpy as jnp
from jax import lax
from jax.experimental import pallas as pl
from jax.experimental.pallas import tpu as pltpu
from jax.sharding import PartitionSpec as P

VARS = 5
CUTS = 2
SUB = 8
VMEM = pl.BlockSpec(memory_space=pltpu.VMEM)
SMEM = pl.BlockSpec(memory_space=pltpu.SMEM)


def params(mib):
    return pltpu.CompilerParams(vmem_limit_bytes=mib * 2**20)


def ceil_to(value, unit):
    return -(-value // unit) * unit


def mixing_matrix(matrix, inst_dev, rows, cols):
    count = matrix.shape[0]
    high = lax.Precision.HIGHEST
    row_id = lax.broadcasted_iota(jnp.int32, (rows, count), 0)
    pick_row = (row_id // SUB == lax.broadcasted_iota(jnp.int32, (rows, count), 1)).astype(jnp.float32)
    col_id = lax.broadcasted_iota(jnp.int32, (count, cols), 1)
    pick_col = (col_id // VARS == lax.broadcasted_iota(jnp.int32, (count, cols), 0)).astype(jnp.float32)
    spread = jnp.dot(
        pick_row,
        jnp.dot(matrix, pick_col, precision=high, preferred_element_type=jnp.float32),
        precision=high,
        preferred_element_type=jnp.float32,
    )
    row_id = lax.broadcasted_iota(jnp.int32, (rows, cols), 0)
    col_var = lax.rem(lax.broadcasted_iota(jnp.int32, (rows, cols), 1), VARS)
    row_var = lax.rem(lax.rem(row_id, SUB) + VARS * SUB * count - VARS * (row_id // SUB), SUB)
    return jnp.where(row_var == col_var, spread, 0.0)


def pack_kernel(count, donor_ref, weights_ref, sent_ref, held, weights, packed, weights_sem, in_sems, out_sems):
    inst_dev, span = donor_ref.shape[1], donor_ref.shape[3]
    depth = inst_dev * VARS
    step = span // CUTS
    fetched = pltpu.make_async_copy(weights_ref, weights, weights_sem)
    pieces = [(r, c) for r in range(2) for c in range(CUTS)]

    def arrival(r, c):
        part = pl.ds(c * step, step)
        return pltpu.make_async_copy(donor_ref.at[1 - r, :, :, part], held.at[r, :, :, part], in_sems.at[r, c])

    def departure(r, c):
        part = pl.ds((r * span + c * step) * depth, step * depth)
        return pltpu.make_async_copy(packed.at[part], sent_ref.at[part], out_sems.at[r, c])

    for r, c in pieces:
        arrival(r, c).start()
    fetched.start()
    fetched.wait()
    spare = lax.axis_index("inst") == -(-count // inst_dev)
    for r, c in pieces:
        arrival(r, c).wait()
        first = (r * span + c * step) * depth
        for k in range(inst_dev):
            for v in range(VARS):
                faces = held[r, k, v, c * step : (c + 1) * step]
                member = k * VARS + v
                if member < weights.shape[1]:
                    faces = jnp.where(spare, weights[r, member : member + 1, :], faces)
                packed[pl.ds(first + member, step, stride=depth), :] = faces
        departure(r, c).start()
    for r, c in pieces:
        departure(r, c).wait()


def prepare_kernel(half, inst_dev, period, time_shift_ref, face_shift_ref, offsets_ref, mix_ref, starts_ref):
    row = half()
    sign = 1 - 2 * row
    count, members = face_shift_ref.shape[0], offsets_ref.shape[1]
    for m in range(count):
        for member in range(members):
            start = sign * face_shift_ref[m] + offsets_ref[row, member]
            starts_ref[m * members + member] = jnp.where(start < 0, start + period, start)
    mix_ref[...] = mixing_matrix(time_shift_ref[row], inst_dev, *mix_ref.shape)


def split(x):
    high = x.astype(jnp.bfloat16)
    return high, (x - high.astype(jnp.float32)).astype(jnp.bfloat16)


def transfer_kernel(inst_dev, blocks, members, got_ref, mix_ref, starts_ref, sent_ref, mixed_ref, weight_ref):
    count = starts_ref.shape[0] // members
    lanes = got_ref.shape[1]
    depth = got_ref.shape[0] // blocks
    spare = -(-count // inst_dev) * inst_dev * VARS
    used = mix_ref.shape[1]
    mix_high, mix_low = split(mix_ref[...])
    mix = jnp.concatenate([mix_high, mix_high], axis=1)
    for block in range(blocks):
        if block % 2 == 0:
            two = [got_ref[b * depth : b * depth + used, :] for b in (block, block + 1)]
            high, low = split(jnp.concatenate(two, axis=1))
            part = jnp.dot(mix, jnp.concatenate([high, low], axis=0), preferred_element_type=jnp.float32) + jnp.dot(mix_low, high, preferred_element_type=jnp.float32)
            for b in range(2):
                one = part[:, b * lanes : (b + 1) * lanes]
                mixed_ref[block + b] = one
                mixed_ref[block + b + blocks] = one
        for member in range(members):
            at = block * depth + spare + member
            weight_ref[member, block] = jnp.broadcast_to(got_ref[at : at + 1, :], (SUB, lanes))
    lane = lax.broadcasted_iota(jnp.int32, (1, 1, lanes), 2)
    sub = lax.broadcasted_iota(jnp.int32, (1, SUB, 1), 1)

    def interpolated(m):
        total = None
        for member in range(members):
            start = starts_ref[m * members + member]
            skip, turn = start // lanes, lax.rem(start, lanes)
            window = mixed_ref[pl.ds(skip, blocks + 1), m * SUB : (m + 1) * SUB, :]
            turned = pltpu.roll(window.reshape((blocks + 1) * SUB, lanes), lax.rem(lanes - turn, lanes), 1)
            turned = turned.reshape(blocks + 1, SUB, lanes)
            term = weight_ref[member] * jnp.where(lane < lanes - turn, turned[:blocks], turned[1:])
            total = term if total is None else total + term
        return total

    parts = {}
    for tile in range(depth // SUB):
        first, last = tile * SUB // VARS, (tile * SUB + SUB - 1) // VARS
        joined = None
        for m in range(first, last + 1):
            if m >= count:
                part = jnp.zeros((blocks, SUB, lanes), jnp.float32)
            else:
                if m not in parts:
                    parts = {m - 1: parts[m - 1], m: interpolated(m)} if m - 1 in parts else {m: interpolated(m)}
                part = parts[m]
            joined = part if joined is None else jnp.where(sub >= m * VARS - tile * SUB, part, joined)
        sent_ref[:, tile * SUB : (tile + 1) * SUB, :] = joined


def unpack_kernel(got_ref, received_ref):
    inst_dev, span = received_ref.shape[1], received_ref.shape[3]
    depth = inst_dev * VARS
    first = pl.program_id(0) * span * depth
    for k in range(inst_dev):
        for v in range(VARS):
            received_ref[0, k, v] = got_ref[pl.ds(first + k * VARS + v, span, stride=depth), :]


def my_row(peers, owners):
    return (lax.axis_index("pitch") * owners + lax.axis_index("inst")) // (peers // 2)


def on_device(donor_state, time_shift, face_shift, weights, offsets, blocks=None, owners=None, exchange=None):
    _, inst_dev, _, span, lanes = donor_state.shape
    blocks, owners = blocks or lax.axis_size("pitch"), owners or lax.axis_size("inst")
    peers = blocks * owners
    members, count = weights.shape[1], time_shift.shape[1]
    depth = inst_dev * VARS
    used = ceil_to(count * VARS, SUB)
    half = functools.partial(my_row, peers, owners)

    def exchanged(x):
        whole = x.reshape(peers, depth, 1, lanes)
        return lax.all_to_all(whole, ("pitch", "inst"), 0, 0, tiled=True).reshape(peers * depth, lanes)

    exchanged = exchange or exchanged

    hbm = pl.BlockSpec(memory_space=pltpu.HBM)
    packed = pl.pallas_call(
        functools.partial(pack_kernel, count),
        out_shape=jax.ShapeDtypeStruct((peers * depth, lanes), jnp.float32),
        in_specs=[hbm] * 2,
        out_specs=hbm,
        scratch_shapes=[
            pltpu.VMEM(donor_state.shape, jnp.float32),
            pltpu.VMEM(weights.shape, jnp.float32),
            pltpu.VMEM((peers * depth, lanes), jnp.float32),
            pltpu.SemaphoreType.DMA(()),
            pltpu.SemaphoreType.DMA((2, CUTS)),
            pltpu.SemaphoreType.DMA((2, CUTS)),
        ],
        compiler_params=params(56),
    )(donor_state, weights)
    mix, starts = pl.pallas_call(
        functools.partial(prepare_kernel, half, inst_dev, blocks * lanes),
        out_shape=(
            jax.ShapeDtypeStruct((count * SUB, used), jnp.float32),
            jax.ShapeDtypeStruct((count * members,), jnp.int32),
        ),
        in_specs=[VMEM, SMEM, SMEM],
        out_specs=(VMEM, SMEM),
        compiler_params=params(8),
    )(time_shift, face_shift, offsets)
    got = exchanged(packed)
    sent = pl.pallas_call(
        functools.partial(transfer_kernel, inst_dev, blocks, members),
        out_shape=jax.ShapeDtypeStruct((blocks, owners * depth, lanes), jnp.float32),
        in_specs=[VMEM, VMEM, SMEM],
        out_specs=VMEM,
        scratch_shapes=[
            pltpu.VMEM((2 * blocks, count * SUB, lanes), jnp.float32),
            pltpu.VMEM((members, blocks, SUB, lanes), jnp.float32),
        ],
        compiler_params=params(24),
    )(got, mix, starts)
    back = exchanged(sent)
    return pl.pallas_call(
        unpack_kernel,
        grid=(2,),
        out_shape=jax.ShapeDtypeStruct(donor_state.shape, jnp.float32),
        in_specs=[VMEM],
        out_specs=pl.BlockSpec((1, inst_dev, VARS, span, lanes), lambda r: (r, 0, 0, 0, 0)),
        compiler_params=params(8),
    )(back)


def solution(mesh):
    return jax.shard_map(
        on_device,
        mesh=mesh,
        in_specs=(P(None, "inst", None, "span", "pitch"), P(), P(), P(None, None, "pitch"), P()),
        out_specs=P(None, "inst", None, "span", "pitch"),
        check_vma=False,
    )
```

```python
import functools

import jax
import jax.numpy as jnp
from jax import lax
from jax.experimental import pallas as pl
from jax.experimental.pallas import tpu as pltpu
from jax.sharding import PartitionSpec as P

VARS = 5
CUTS = 2
SUB = 8
VMEM = pl.BlockSpec(memory_space=pltpu.VMEM)
SMEM = pl.BlockSpec(memory_space=pltpu.SMEM)


def params(mib):
    return pltpu.CompilerParams(vmem_limit_bytes=mib * 2**20)


def ceil_to(value, unit):
    return -(-value // unit) * unit


def mixing_matrix(matrix, size):
    count = matrix.shape[0]
    high = lax.Precision.HIGHEST

    def picks(shape, dim):
        own = lax.broadcasted_iota(jnp.int32, shape, dim) // VARS
        return (own == lax.broadcasted_iota(jnp.int32, shape, 1 - dim)).astype(jnp.float32)

    spread = jnp.dot(
        picks((size, count), 0),
        jnp.dot(matrix, picks((count, size), 1), precision=high, preferred_element_type=jnp.float32),
        precision=high,
        preferred_element_type=jnp.float32,
    )
    row_var, col_var = (lax.rem(lax.broadcasted_iota(jnp.int32, (size, size), d), VARS) for d in range(2))
    return jnp.where(row_var == col_var, spread, 0.0)


def pack_kernel(count, donor_ref, weights_ref, sent_ref, held, weights, packed, weights_sem, in_sems, out_sems):
    inst_dev, span = donor_ref.shape[1], donor_ref.shape[3]
    depth = inst_dev * VARS
    step = span // CUTS
    fetched = pltpu.make_async_copy(weights_ref, weights, weights_sem)
    pieces = [(r, c) for r in range(2) for c in range(CUTS)]

    def arrival(r, c):
        part = pl.ds(c * step, step)
        return pltpu.make_async_copy(donor_ref.at[1 - r, :, :, part], held.at[r, :, :, part], in_sems.at[r, c])

    def departure(r, c):
        part = pl.ds((r * span + c * step) * depth, step * depth)
        return pltpu.make_async_copy(packed.at[part], sent_ref.at[part], out_sems.at[r, c])

    for r, c in pieces:
        arrival(r, c).start()
    fetched.start()
    fetched.wait()
    spare = lax.axis_index("inst") == -(-count // inst_dev)
    for r, c in pieces:
        arrival(r, c).wait()
        first = (r * span + c * step) * depth
        for k in range(inst_dev):
            for v in range(VARS):
                faces = held[r, k, v, c * step : (c + 1) * step]
                member = k * VARS + v
                if member < weights.shape[1]:
                    faces = jnp.where(spare, weights[r, member : member + 1, :], faces)
                packed[pl.ds(first + member, step, stride=depth), :] = faces
        departure(r, c).start()
    for r, c in pieces:
        departure(r, c).wait()


def prepare_kernel(half, lanes, period, time_shift_ref, face_shift_ref, offsets_ref, mix_ref, starts_ref):
    row = half()
    sign = 1 - 2 * row
    count, members = face_shift_ref.shape[0], offsets_ref.shape[1]
    for m in range(count):
        for member in range(members):
            start = sign * face_shift_ref[m] + offsets_ref[row, member]
            start = jnp.where(start < 0, start + period, start)
            starts_ref[m * members + member] = lax.div(start, lanes)
            starts_ref[(count + m) * members + member] = lax.rem(start, lanes)
    mix_ref[...] = mixing_matrix(time_shift_ref[row], mix_ref.shape[0])


def split(x):
    high = x.astype(jnp.bfloat16)
    return high, (x - high.astype(jnp.float32)).astype(jnp.bfloat16)


def transfer_kernel(inst_dev, blocks, members, got_ref, mix_ref, table_ref, sent_ref, mixed_ref, starts_ref, sem):
    table = pltpu.make_async_copy(table_ref, starts_ref, sem)
    table.start()
    count = starts_ref.shape[0] // (2 * members)
    lanes = got_ref.shape[1]
    depth = got_ref.shape[0] // blocks
    twice = 2 * blocks + 1
    used = mix_ref.shape[0]
    mix_high, mix_low = split(mix_ref[...])
    mix = jnp.concatenate([mix_high, mix_high], axis=1)
    for block in range(0, blocks, 2):
        high, low = split(jnp.concatenate([got_ref[b * depth : b * depth + used, :] for b in (block, block + 1)], axis=1))
        part = jnp.dot(mix, jnp.concatenate([high, low], axis=0), preferred_element_type=jnp.float32)
        part = part + jnp.dot(mix_low, high, preferred_element_type=jnp.float32)
        for b in range(2):
            one = part[:, b * lanes : (b + 1) * lanes]
            for copy in range(2):
                mixed_ref[pl.ds(block + b + copy * blocks, used, stride=twice), :] = one
    table.wait()
    first_spare = -(-count // inst_dev) * inst_dev * VARS
    weights = [got_ref[pl.ds(first_spare + member, blocks, stride=depth), :] for member in range(members)]
    lane = lax.broadcasted_iota(jnp.int32, (blocks, lanes), 1)
    for m in range(count):
        totals = [None] * VARS
        for member in range(members):
            skip, turn = starts_ref[m * members + member], starts_ref[(count + m) * members + member]
            back = jnp.where(turn == 0, 0, lanes - turn)
            here = lane >= turn
            for v in range(VARS):
                at = (m * VARS + v) * twice + skip
                faces = jnp.where(here, mixed_ref[pl.ds(at, blocks), :], mixed_ref[pl.ds(at + 1, blocks), :])
                term = weights[member] * pltpu.roll(faces, back, 1)
                totals[v] = term if member == 0 else totals[v] + term
        for v in range(VARS):
            sent_ref[pl.ds(m * VARS + v, blocks, stride=depth), :] = totals[v]
    none = jnp.zeros((depth - count * VARS, lanes), jnp.float32)
    for block in range(blocks):
        sent_ref[block * depth + count * VARS : (block + 1) * depth, :] = none


def unpack_kernel(got_ref, received_ref):
    inst_dev, span = received_ref.shape[1], received_ref.shape[3]
    depth = inst_dev * VARS
    first = pl.program_id(0) * span * depth
    for k in range(inst_dev):
        for v in range(VARS):
            received_ref[0, k, v] = got_ref[pl.ds(first + k * VARS + v, span, stride=depth), :]


def my_row(peers, owners):
    return (lax.axis_index("pitch") * owners + lax.axis_index("inst")) // (peers // 2)


def on_device(donor_state, time_shift, face_shift, weights, offsets, blocks=None, owners=None, exchange=None):
    _, inst_dev, _, span, lanes = donor_state.shape
    blocks, owners = blocks or lax.axis_size("pitch"), owners or lax.axis_size("inst")
    peers = blocks * owners
    members, count = weights.shape[1], time_shift.shape[1]
    depth = inst_dev * VARS
    used = ceil_to(count * VARS, SUB)
    half = functools.partial(my_row, peers, owners)

    def exchanged(x):
        whole = x.reshape(peers, depth, 1, lanes)
        return lax.all_to_all(whole, ("pitch", "inst"), 0, 0, tiled=True).reshape(peers * depth, lanes)

    exchanged = exchange or exchanged

    hbm = pl.BlockSpec(memory_space=pltpu.HBM)
    packed = pl.pallas_call(
        functools.partial(pack_kernel, count),
        out_shape=jax.ShapeDtypeStruct((peers * depth, lanes), jnp.float32),
        in_specs=[hbm] * 2,
        out_specs=hbm,
        scratch_shapes=[
            pltpu.VMEM(donor_state.shape, jnp.float32),
            pltpu.VMEM(weights.shape, jnp.float32),
            pltpu.VMEM((peers * depth, lanes), jnp.float32),
            pltpu.SemaphoreType.DMA(()),
            pltpu.SemaphoreType.DMA((2, CUTS)),
            pltpu.SemaphoreType.DMA((2, CUTS)),
        ],
        compiler_params=params(56),
    )(donor_state, weights)
    mix, starts = pl.pallas_call(
        functools.partial(prepare_kernel, half, lanes, blocks * lanes),
        out_shape=(
            jax.ShapeDtypeStruct((used, used), jnp.float32),
            jax.ShapeDtypeStruct((2 * count * members,), jnp.int32),
        ),
        in_specs=[VMEM, SMEM, SMEM],
        out_specs=(VMEM, SMEM),
        compiler_params=params(8),
    )(time_shift, face_shift, offsets)
    got = exchanged(packed)
    sent = pl.pallas_call(
        functools.partial(transfer_kernel, inst_dev, blocks, members),
        out_shape=jax.ShapeDtypeStruct((peers * depth, lanes), jnp.float32),
        in_specs=[VMEM, VMEM, VMEM],
        out_specs=VMEM,
        scratch_shapes=[
            pltpu.VMEM((used * (2 * blocks + 1), lanes), jnp.float32),
            pltpu.SMEM((2 * count * members,), jnp.int32),
            pltpu.SemaphoreType.DMA(()),
        ],
        compiler_params=params(24),
    )(got, mix, starts)
    back = exchanged(sent)
    return pl.pallas_call(
        unpack_kernel,
        grid=(2,),
        out_shape=jax.ShapeDtypeStruct(donor_state.shape, jnp.float32),
        in_specs=[VMEM],
        out_specs=pl.BlockSpec((1, inst_dev, VARS, span, lanes), lambda r: (r, 0, 0, 0, 0)),
        compiler_params=params(8),
    )(back)


def solution(mesh):
    return jax.shard_map(
        on_device,
        mesh=mesh,
        in_specs=(P(None, "inst", None, "span", "pitch"), P(), P(), P(None, None, "pitch"), P()),
        out_specs=P(None, "inst", None, "span", "pitch"),
        check_vma=False,
    )
```

```python
import functools

import jax
import jax.numpy as jnp
from jax import lax
from jax.experimental import pallas as pl
from jax.experimental.pallas import tpu as pltpu
from jax.sharding import PartitionSpec as P

VARS = 5
CUTS = 1
TILE = 16
VMEM = pl.BlockSpec(memory_space=pltpu.VMEM)
SMEM = pl.BlockSpec(memory_space=pltpu.SMEM)


def params(mib):
    return pltpu.CompilerParams(vmem_limit_bytes=mib * 2**20)


def ceil_to(value, unit):
    return -(-value // unit) * unit


def mixing_matrix(matrix, size):
    count = matrix.shape[0]
    high = lax.Precision.HIGHEST

    def picks(shape, dim):
        own = lax.broadcasted_iota(jnp.int32, shape, dim) // VARS
        return (own == lax.broadcasted_iota(jnp.int32, shape, 1 - dim)).astype(jnp.float32)

    spread = jnp.dot(
        picks((size, count), 0),
        jnp.dot(matrix, picks((count, size), 1), precision=high, preferred_element_type=jnp.float32),
        precision=high,
        preferred_element_type=jnp.float32,
    )
    row_var, col_var = (lax.rem(lax.broadcasted_iota(jnp.int32, (size, size), d), VARS) for d in range(2))
    return jnp.where(row_var == col_var, spread, 0.0)


def pack_kernel(count, donor_ref, weights_ref, sent_ref, held, weights, packed, weights_sem, in_sems, out_sems):
    inst_dev, span = donor_ref.shape[1], donor_ref.shape[3]
    depth = inst_dev * VARS
    step = span // CUTS
    fetched = pltpu.make_async_copy(weights_ref, weights, weights_sem)
    pieces = [(r, c) for r in range(2) for c in range(CUTS)]

    def arrival(r, c):
        part = pl.ds(c * step, step)
        return pltpu.make_async_copy(donor_ref.at[1 - r, :, :, part], held.at[r, :, :, part], in_sems.at[r, c])

    def departure(r, c):
        part = pl.ds((r * span + c * step) * depth, step * depth)
        return pltpu.make_async_copy(packed.at[part], sent_ref.at[part], out_sems.at[r, c])

    for r, c in pieces:
        arrival(r, c).start()
    fetched.start()
    fetched.wait()
    spare = lax.axis_index("inst") == -(-count // inst_dev)
    for r, c in pieces:
        arrival(r, c).wait()
        first = (r * span + c * step) * depth
        for k in range(inst_dev):
            for v in range(VARS):
                faces = held[r, k, v, c * step : (c + 1) * step]
                member = k * VARS + v
                if member < weights.shape[1]:
                    faces = jnp.where(spare, weights[r, member : member + 1, :], faces)
                packed[pl.ds(first + member, step, stride=depth), :] = faces
        departure(r, c).start()
    for r, c in pieces:
        departure(r, c).wait()


def prepare_kernel(half, lanes, period, time_shift_ref, face_shift_ref, offsets_ref, mix_ref, starts_ref):
    row = half()
    sign = 1 - 2 * row
    count, members = face_shift_ref.shape[0], offsets_ref.shape[1]
    for m in range(count):
        for member in range(members):
            start = sign * face_shift_ref[m] + offsets_ref[row, member]
            start = jnp.where(start < 0, start + period, start)
            starts_ref[m * members + member] = lax.div(start, lanes)
            starts_ref[(count + m) * members + member] = lax.rem(start, lanes)
    mix_ref[...] = mixing_matrix(time_shift_ref[row], mix_ref.shape[0])


def split(x):
    high = x.astype(jnp.bfloat16)
    return high, (x - high.astype(jnp.float32)).astype(jnp.bfloat16)


def transfer_kernel(inst_dev, blocks, members, got_ref, mix_ref, table_ref, sent_ref, mixed_ref, starts_ref, sem):
    table = pltpu.make_async_copy(table_ref, starts_ref, sem)
    table.start()
    count = starts_ref.shape[0] // (2 * members)
    lanes = got_ref.shape[1]
    depth = got_ref.shape[0] // blocks
    twice = 2 * blocks + 1
    used = mix_ref.shape[0]
    mix_high, mix_low = split(mix_ref[...])
    for block in range(0, blocks, 2):
        high, low = split(jnp.concatenate([got_ref[b * depth : b * depth + used, :] for b in (block, block + 1)], axis=1))
        part = jnp.dot(mix_high, high, preferred_element_type=jnp.float32)
        part = part + jnp.dot(mix_high, low, preferred_element_type=jnp.float32)
        part = part + jnp.dot(mix_low, high, preferred_element_type=jnp.float32)
        for b in range(2):
            one = part[:, b * lanes : (b + 1) * lanes]
            for copy in range(2):
                mixed_ref[pl.ds(block + b + copy * blocks, used, stride=twice), :] = one
    table.wait()
    first_spare = -(-count // inst_dev) * inst_dev * VARS
    weights = [got_ref[pl.ds(first_spare + member, blocks, stride=depth), :] for member in range(members)]
    lane = lax.broadcasted_iota(jnp.int32, (blocks, lanes), 1)
    for m in range(count):
        totals = [None] * VARS
        for member in range(members):
            skip, turn = starts_ref[m * members + member], starts_ref[(count + m) * members + member]
            back = jnp.where(turn == 0, 0, lanes - turn)
            here = lane >= turn
            for v in range(VARS):
                at = (m * VARS + v) * twice + skip
                faces = jnp.where(here, mixed_ref[pl.ds(at, blocks), :], mixed_ref[pl.ds(at + 1, blocks), :])
                term = weights[member] * pltpu.roll(faces, back, 1)
                totals[v] = term if member == 0 else totals[v] + term
        for v in range(VARS):
            sent_ref[pl.ds(m * VARS + v, blocks, stride=depth), :] = totals[v]
    none = jnp.zeros((depth - count * VARS, lanes), jnp.float32)
    for block in range(blocks):
        sent_ref[block * depth + count * VARS : (block + 1) * depth, :] = none


def unpack_kernel(got_ref, received_ref):
    inst_dev, span = received_ref.shape[1], received_ref.shape[3]
    depth = inst_dev * VARS
    first = pl.program_id(0) * span * depth
    for k in range(inst_dev):
        for v in range(VARS):
            received_ref[0, k, v] = got_ref[pl.ds(first + k * VARS + v, span, stride=depth), :]


def my_row(peers, owners):
    return (lax.axis_index("pitch") * owners + lax.axis_index("inst")) // (peers // 2)


def on_device(donor_state, time_shift, face_shift, weights, offsets, blocks=None, owners=None, exchange=None):
    _, inst_dev, _, span, lanes = donor_state.shape
    blocks, owners = blocks or lax.axis_size("pitch"), owners or lax.axis_size("inst")
    peers = blocks * owners
    members, count = weights.shape[1], time_shift.shape[1]
    depth = inst_dev * VARS
    used = ceil_to(count * VARS, TILE)
    half = functools.partial(my_row, peers, owners)

    def exchanged(x):
        whole = x.reshape(peers, depth, 1, lanes)
        return lax.all_to_all(whole, ("pitch", "inst"), 0, 0, tiled=True).reshape(peers * depth, lanes)

    exchanged = exchange or exchanged

    hbm = pl.BlockSpec(memory_space=pltpu.HBM)
    packed = pl.pallas_call(
        functools.partial(pack_kernel, count),
        out_shape=jax.ShapeDtypeStruct((peers * depth, lanes), jnp.float32),
        in_specs=[hbm] * 2,
        out_specs=hbm,
        scratch_shapes=[
            pltpu.VMEM(donor_state.shape, jnp.float32),
            pltpu.VMEM(weights.shape, jnp.float32),
            pltpu.VMEM((peers * depth, lanes), jnp.float32),
            pltpu.SemaphoreType.DMA(()),
            pltpu.SemaphoreType.DMA((2, CUTS)),
            pltpu.SemaphoreType.DMA((2, CUTS)),
        ],
        compiler_params=params(56),
    )(donor_state, weights)
    mix, starts = pl.pallas_call(
        functools.partial(prepare_kernel, half, lanes, blocks * lanes),
        out_shape=(
            jax.ShapeDtypeStruct((used, used), jnp.float32),
            jax.ShapeDtypeStruct((2 * count * members,), jnp.int32),
        ),
        in_specs=[VMEM, SMEM, SMEM],
        out_specs=(VMEM, SMEM),
        compiler_params=params(8),
    )(time_shift, face_shift, offsets)
    got = exchanged(packed)
    sent = pl.pallas_call(
        functools.partial(transfer_kernel, inst_dev, blocks, members),
        out_shape=jax.ShapeDtypeStruct((peers * depth, lanes), jnp.float32),
        in_specs=[VMEM, VMEM, VMEM],
        out_specs=VMEM,
        scratch_shapes=[
            pltpu.VMEM((used * (2 * blocks + 1), lanes), jnp.float32),
            pltpu.SMEM((2 * count * members,), jnp.int32),
            pltpu.SemaphoreType.DMA(()),
        ],
        compiler_params=params(24),
    )(got, mix, starts)
    back = exchanged(sent)
    return pl.pallas_call(
        unpack_kernel,
        grid=(2,),
        out_shape=jax.ShapeDtypeStruct(donor_state.shape, jnp.float32),
        in_specs=[VMEM],
        out_specs=pl.BlockSpec((1, inst_dev, VARS, span, lanes), lambda r: (r, 0, 0, 0, 0)),
        compiler_params=params(8),
    )(back)


def solution(mesh):
    return jax.shard_map(
        on_device,
        mesh=mesh,
        in_specs=(P(None, "inst", None, "span", "pitch"), P(), P(), P(None, None, "pitch"), P()),
        out_specs=P(None, "inst", None, "span", "pitch"),
        check_vma=False,
    )
```

```python
import functools

import jax
import jax.numpy as jnp
from jax import lax
from jax.experimental import pallas as pl
from jax.experimental.pallas import tpu as pltpu
from jax.sharding import PartitionSpec as P

VARS = 5
CUTS = 1
TILE = 16
VMEM = pl.BlockSpec(memory_space=pltpu.VMEM)
SMEM = pl.BlockSpec(memory_space=pltpu.SMEM)


def params(mib):
    return pltpu.CompilerParams(vmem_limit_bytes=mib * 2**20)


def ceil_to(value, unit):
    return -(-value // unit) * unit


def mixing_matrix(matrix, size):
    count = matrix.shape[0]
    high = lax.Precision.HIGHEST

    def picks(shape, dim):
        own = lax.broadcasted_iota(jnp.int32, shape, dim) // VARS
        return (own == lax.broadcasted_iota(jnp.int32, shape, 1 - dim)).astype(jnp.float32)

    spread = jnp.dot(
        picks((size, count), 0),
        jnp.dot(matrix, picks((count, size), 1), precision=high, preferred_element_type=jnp.float32),
        precision=high,
        preferred_element_type=jnp.float32,
    )
    row_var, col_var = (lax.rem(lax.broadcasted_iota(jnp.int32, (size, size), d), VARS) for d in range(2))
    return jnp.where(row_var == col_var, spread, 0.0)


def pack_kernel(count, donor_ref, weights_ref, sent_ref, held, weights, packed, weights_sem, in_sems, out_sems):
    inst_dev, span = donor_ref.shape[1], donor_ref.shape[3]
    depth = inst_dev * VARS
    step = span // CUTS
    fetched = pltpu.make_async_copy(weights_ref, weights, weights_sem)
    pieces = [(r, c) for r in range(2) for c in range(CUTS)]

    def arrival(r, c):
        part = pl.ds(c * step, step)
        return pltpu.make_async_copy(donor_ref.at[1 - r, :, :, part], held.at[r, :, :, part], in_sems.at[r, c])

    def departure(r, c):
        part = pl.ds((r * span + c * step) * depth, step * depth)
        return pltpu.make_async_copy(packed.at[part], sent_ref.at[part], out_sems.at[r, c])

    for r, c in pieces:
        arrival(r, c).start()
    fetched.start()
    fetched.wait()
    spare = lax.axis_index("inst") == -(-count // inst_dev)
    for r, c in pieces:
        arrival(r, c).wait()
        first = (r * span + c * step) * depth
        for k in range(inst_dev):
            for v in range(VARS):
                faces = held[r, k, v, c * step : (c + 1) * step]
                member = k * VARS + v
                if member < weights.shape[1]:
                    faces = jnp.where(spare, weights[r, member : member + 1, :], faces)
                packed[pl.ds(first + member, step, stride=depth), :] = faces
        departure(r, c).start()
    for r, c in pieces:
        departure(r, c).wait()


def prepare_kernel(half, lanes, period, time_shift_ref, face_shift_ref, offsets_ref, mix_ref, starts_ref):
    row = half()
    sign = 1 - 2 * row
    count, members = face_shift_ref.shape[0], offsets_ref.shape[1]
    for m in range(count):
        for member in range(members):
            start = sign * face_shift_ref[m] + offsets_ref[row, member]
            start = jnp.where(start < 0, start + period, start)
            starts_ref[m * members + member] = lax.div(start, lanes)
            starts_ref[(count + m) * members + member] = lax.rem(start, lanes)
    mix_ref[...] = mixing_matrix(time_shift_ref[row], mix_ref.shape[0])


def split(x):
    high = x.astype(jnp.bfloat16)
    return high, (x - high.astype(jnp.float32)).astype(jnp.bfloat16)


def transfer_kernel(inst_dev, blocks, members, got_ref, mix_ref, table_ref, sent_ref, mixed_ref, starts_ref, sem):
    table = pltpu.make_async_copy(table_ref, starts_ref, sem)
    table.start()
    count = starts_ref.shape[0] // (2 * members)
    lanes = got_ref.shape[1]
    depth = got_ref.shape[0] // blocks
    twice = 2 * blocks + 1
    used = mix_ref.shape[0]
    mix_high, mix_low = split(mix_ref[...])
    for block in range(0, blocks, 2):
        high, low = split(jnp.concatenate([got_ref[b * depth : b * depth + used, :] for b in (block, block + 1)], axis=1))
        part = jnp.dot(mix_high, high, preferred_element_type=jnp.float32)
        part = part + jnp.dot(mix_high, low, preferred_element_type=jnp.float32)
        part = part + jnp.dot(mix_low, high, preferred_element_type=jnp.float32)
        for b in range(2):
            one = part[:, b * lanes : (b + 1) * lanes]
            for copy in range(2):
                mixed_ref[pl.ds(block + b + copy * blocks, used, stride=twice), :] = one
    table.wait()
    first_spare = -(-count // inst_dev) * inst_dev * VARS
    weights = [got_ref[pl.ds(first_spare + member, blocks, stride=depth), :] for member in range(members)]
    lane = lax.broadcasted_iota(jnp.int32, (blocks, lanes), 1)

    def place(m, v):
        owner, own = divmod(m * VARS + v, inst_dev * VARS)
        return pl.ds(owner * blocks * inst_dev * VARS + own, blocks, stride=inst_dev * VARS)

    for m in range(count):
        totals = [None] * VARS
        for member in range(members):
            skip, turn = starts_ref[m * members + member], starts_ref[(count + m) * members + member]
            back = jnp.where(turn == 0, 0, lanes - turn)
            here = lane >= turn
            for v in range(VARS):
                at = (m * VARS + v) * twice + skip
                faces = jnp.where(here, mixed_ref[pl.ds(at, blocks), :], mixed_ref[pl.ds(at + 1, blocks), :])
                term = weights[member] * pltpu.roll(faces, back, 1)
                totals[v] = term if member == 0 else totals[v] + term
        for v in range(VARS):
            sent_ref[place(m, v), :] = totals[v]
    none = jnp.zeros((blocks, lanes), jnp.float32)
    for m in range(count, depth // VARS):
        for v in range(VARS):
            sent_ref[place(m, v), :] = none


def unpack_kernel(blocks, owners, got_ref, received_ref):
    inst_dev, span = received_ref.shape[1], received_ref.shape[3]
    depth = inst_dev * VARS
    first = pl.program_id(0) * (span // owners)
    for c in range(span // owners):
        for k in range(inst_dev):
            for v in range(VARS):
                rows = pl.ds((first + c) * depth + k * VARS + v, owners, stride=blocks * depth)
                received_ref[0, k, v, c * owners : (c + 1) * owners] = got_ref[rows, :]


def my_row(peers, owners):
    return (lax.axis_index("pitch") * owners + lax.axis_index("inst")) // (peers // 2)


def on_device(donor_state, time_shift, face_shift, weights, offsets, blocks=None, owners=None, exchange=None):
    _, inst_dev, _, span, lanes = donor_state.shape
    blocks, owners = blocks or lax.axis_size("pitch"), owners or lax.axis_size("inst")
    peers = blocks * owners
    members, count = weights.shape[1], time_shift.shape[1]
    depth = inst_dev * VARS
    used = ceil_to(count * VARS, TILE)
    half = functools.partial(my_row, peers, owners)

    def exchanged(x, axes):
        whole = x.reshape(peers, depth, 1, lanes)
        return lax.all_to_all(whole, axes, 0, 0, tiled=True).reshape(peers * depth, lanes)

    exchanged = exchange or exchanged

    hbm = pl.BlockSpec(memory_space=pltpu.HBM)
    packed = pl.pallas_call(
        functools.partial(pack_kernel, count),
        out_shape=jax.ShapeDtypeStruct((peers * depth, lanes), jnp.float32),
        in_specs=[hbm] * 2,
        out_specs=hbm,
        scratch_shapes=[
            pltpu.VMEM(donor_state.shape, jnp.float32),
            pltpu.VMEM(weights.shape, jnp.float32),
            pltpu.VMEM((peers * depth, lanes), jnp.float32),
            pltpu.SemaphoreType.DMA(()),
            pltpu.SemaphoreType.DMA((2, CUTS)),
            pltpu.SemaphoreType.DMA((2, CUTS)),
        ],
        compiler_params=params(56),
    )(donor_state, weights)
    mix, starts = pl.pallas_call(
        functools.partial(prepare_kernel, half, lanes, blocks * lanes),
        out_shape=(
            jax.ShapeDtypeStruct((used, used), jnp.float32),
            jax.ShapeDtypeStruct((2 * count * members,), jnp.int32),
        ),
        in_specs=[VMEM, SMEM, SMEM],
        out_specs=(VMEM, SMEM),
        compiler_params=params(8),
    )(time_shift, face_shift, offsets)
    got = exchanged(packed, ("pitch", "inst"))
    sent = pl.pallas_call(
        functools.partial(transfer_kernel, inst_dev, blocks, members),
        out_shape=jax.ShapeDtypeStruct((peers * depth, lanes), jnp.float32),
        in_specs=[VMEM, VMEM, VMEM],
        out_specs=VMEM,
        scratch_shapes=[
            pltpu.VMEM((used * (2 * blocks + 1), lanes), jnp.float32),
            pltpu.SMEM((2 * count * members,), jnp.int32),
            pltpu.SemaphoreType.DMA(()),
        ],
        compiler_params=params(24),
    )(got, mix, starts)
    back = exchanged(sent, ("inst", "pitch"))
    return pl.pallas_call(
        functools.partial(unpack_kernel, blocks, owners),
        grid=(2,),
        out_shape=jax.ShapeDtypeStruct(donor_state.shape, jnp.float32),
        in_specs=[VMEM],
        out_specs=pl.BlockSpec((1, inst_dev, VARS, span, lanes), lambda r: (r, 0, 0, 0, 0)),
        compiler_params=params(8),
    )(back)


def solution(mesh):
    return jax.shard_map(
        on_device,
        mesh=mesh,
        in_specs=(P(None, "inst", None, "span", "pitch"), P(), P(), P(None, None, "pitch"), P()),
        out_specs=P(None, "inst", None, "span", "pitch"),
        check_vma=False,
    )
```

```python
import functools

import jax
import jax.numpy as jnp
from jax import lax
from jax.experimental import pallas as pl
from jax.experimental.pallas import tpu as pltpu
from jax.sharding import PartitionSpec as P

VARS = 5
CUTS = 1
TILE = 16
VMEM = pl.BlockSpec(memory_space=pltpu.VMEM)
SMEM = pl.BlockSpec(memory_space=pltpu.SMEM)


def params(mib):
    return pltpu.CompilerParams(vmem_limit_bytes=mib * 2**20)


def ceil_to(value, unit):
    return -(-value // unit) * unit


def mixing_matrix(matrix, size):
    count = matrix.shape[0]
    high = lax.Precision.HIGHEST

    def picks(shape, dim):
        own = lax.broadcasted_iota(jnp.int32, shape, dim) // VARS
        return (own == lax.broadcasted_iota(jnp.int32, shape, 1 - dim)).astype(jnp.float32)

    spread = jnp.dot(
        picks((size, count), 0),
        jnp.dot(matrix, picks((count, size), 1), precision=high, preferred_element_type=jnp.float32),
        precision=high,
        preferred_element_type=jnp.float32,
    )
    row_var, col_var = (lax.rem(lax.broadcasted_iota(jnp.int32, (size, size), d), VARS) for d in range(2))
    return jnp.where(row_var == col_var, spread, 0.0)


def pack_kernel(count, donor_ref, weights_ref, sent_ref, held, weights, packed, weights_sem, in_sems, out_sems):
    inst_dev, span = donor_ref.shape[1], donor_ref.shape[3]
    depth = inst_dev * VARS
    step = span // CUTS
    fetched = pltpu.make_async_copy(weights_ref, weights, weights_sem)
    pieces = [(r, c) for r in range(2) for c in range(CUTS)]

    def arrival(r, c):
        part = pl.ds(c * step, step)
        return pltpu.make_async_copy(donor_ref.at[1 - r, :, :, part], held.at[r, :, :, part], in_sems.at[r, c])

    def departure(r, c):
        part = pl.ds((r * span + c * step) * depth, step * depth)
        return pltpu.make_async_copy(packed.at[part], sent_ref.at[part], out_sems.at[r, c])

    for r, c in pieces:
        arrival(r, c).start()
    fetched.start()
    fetched.wait()
    spare = lax.axis_index("inst") == -(-count // inst_dev)
    for r, c in pieces:
        arrival(r, c).wait()
        first = (r * span + c * step) * depth
        for k in range(inst_dev):
            for v in range(VARS):
                faces = held[r, k, v, c * step : (c + 1) * step]
                member = k * VARS + v
                if member < weights.shape[1]:
                    faces = jnp.where(spare, weights[r, member : member + 1, :], faces)
                packed[pl.ds(first + member, step, stride=depth), :] = faces
        departure(r, c).start()
    for r, c in pieces:
        departure(r, c).wait()


def prepare_kernel(half, lanes, period, time_shift_ref, face_shift_ref, offsets_ref, mix_ref, starts_ref):
    row = half()
    sign = 1 - 2 * row
    count, members = face_shift_ref.shape[0], offsets_ref.shape[1]
    for m in range(count):
        for member in range(members):
            start = sign * face_shift_ref[m] + offsets_ref[row, member]
            start = jnp.where(start < 0, start + period, start)
            starts_ref[m * members + member] = lax.div(start, lanes)
            starts_ref[(count + m) * members + member] = lax.rem(start, lanes)
    mix_ref[...] = mixing_matrix(time_shift_ref[row], mix_ref.shape[0])


def split(x):
    high = x.astype(jnp.bfloat16)
    return high, (x - high.astype(jnp.float32)).astype(jnp.bfloat16)


def transfer_kernel(inst_dev, blocks, members, got_ref, mix_ref, table_ref, sent_ref, mixed_ref, starts_ref, sem):
    table = pltpu.make_async_copy(table_ref, starts_ref, sem)
    table.start()
    count = starts_ref.shape[0] // (2 * members)
    lanes = got_ref.shape[1]
    depth = got_ref.shape[0] // blocks
    twice = 2 * blocks + 1
    used = mix_ref.shape[0]
    mix_high, mix_low = split(mix_ref[...])
    for block in range(0, blocks, 2):
        high, low = split(jnp.concatenate([got_ref[b * depth : b * depth + used, :] for b in (block, block + 1)], axis=1))
        part = jnp.dot(mix_high, high, preferred_element_type=jnp.float32)
        part = part + jnp.dot(mix_high, low, preferred_element_type=jnp.float32)
        part = part + jnp.dot(mix_low, high, preferred_element_type=jnp.float32)
        for b in range(2):
            one = part[:, b * lanes : (b + 1) * lanes]
            for copy in range(2):
                mixed_ref[pl.ds(block + b + copy * blocks, used, stride=twice), :] = one
    table.wait()
    first_spare = -(-count // inst_dev) * inst_dev * VARS
    weights = [got_ref[pl.ds(first_spare + member, blocks, stride=depth), :] for member in range(members)]
    lane = lax.broadcasted_iota(jnp.int32, (blocks, lanes), 1)

    def place(m, v):
        owner, own = divmod(m * VARS + v, inst_dev * VARS)
        return pl.ds(owner * blocks * inst_dev * VARS + own, blocks, stride=inst_dev * VARS)

    for m in range(count):
        totals = [None] * VARS
        for member in range(members):
            skip, turn = starts_ref[m * members + member], starts_ref[(count + m) * members + member]
            back = jnp.where(turn == 0, 0, lanes - turn)
            here = lane >= turn
            for v in range(VARS):
                at = (m * VARS + v) * twice + skip
                faces = jnp.where(here, mixed_ref[pl.ds(at, blocks), :], mixed_ref[pl.ds(at + 1, blocks), :])
                term = weights[member] * pltpu.roll(faces, back, 1)
                totals[v] = term if member == 0 else totals[v] + term
        for v in range(VARS):
            sent_ref[place(m, v), :] = totals[v]
    none = jnp.zeros((blocks, lanes), jnp.float32)
    for m in range(count, depth // VARS):
        for v in range(VARS):
            sent_ref[place(m, v), :] = none


def unpack_kernel(blocks, owners, got_ref, received_ref, held, sems):
    inst_dev, span = received_ref.shape[1], received_ref.shape[3]
    depth = inst_dev * VARS
    parts = [(r, k) for r in range(2) for k in range(inst_dev)]

    def departure(r, k):
        return pltpu.make_async_copy(held.at[r, k], received_ref.at[r, k], sems.at[r, k])

    for r, k in parts:
        for v in range(VARS):
            for c in range(span // owners):
                rows = pl.ds((r * (span // owners) + c) * depth + k * VARS + v, owners, stride=blocks * depth)
                held[r, k, v, c * owners : (c + 1) * owners] = got_ref[rows, :]
        departure(r, k).start()
    for r, k in parts:
        departure(r, k).wait()


def my_row(peers, owners):
    return (lax.axis_index("pitch") * owners + lax.axis_index("inst")) // (peers // 2)


def on_device(donor_state, time_shift, face_shift, weights, offsets, blocks=None, owners=None, exchange=None):
    _, inst_dev, _, span, lanes = donor_state.shape
    blocks, owners = blocks or lax.axis_size("pitch"), owners or lax.axis_size("inst")
    peers = blocks * owners
    members, count = weights.shape[1], time_shift.shape[1]
    depth = inst_dev * VARS
    used = ceil_to(count * VARS, TILE)
    half = functools.partial(my_row, peers, owners)

    def exchanged(x, axes):
        whole = x.reshape(peers, depth, 1, lanes)
        return lax.all_to_all(whole, axes, 0, 0, tiled=True).reshape(peers * depth, lanes)

    exchanged = exchange or exchanged

    hbm = pl.BlockSpec(memory_space=pltpu.HBM)
    packed = pl.pallas_call(
        functools.partial(pack_kernel, count),
        out_shape=jax.ShapeDtypeStruct((peers * depth, lanes), jnp.float32),
        in_specs=[hbm] * 2,
        out_specs=hbm,
        scratch_shapes=[
            pltpu.VMEM(donor_state.shape, jnp.float32),
            pltpu.VMEM(weights.shape, jnp.float32),
            pltpu.VMEM((peers * depth, lanes), jnp.float32),
            pltpu.SemaphoreType.DMA(()),
            pltpu.SemaphoreType.DMA((2, CUTS)),
            pltpu.SemaphoreType.DMA((2, CUTS)),
        ],
        compiler_params=params(56),
    )(donor_state, weights)
    mix, starts = pl.pallas_call(
        functools.partial(prepare_kernel, half, lanes, blocks * lanes),
        out_shape=(
            jax.ShapeDtypeStruct((used, used), jnp.float32),
            jax.ShapeDtypeStruct((2 * count * members,), jnp.int32),
        ),
        in_specs=[VMEM, SMEM, SMEM],
        out_specs=(VMEM, SMEM),
        compiler_params=params(8),
    )(time_shift, face_shift, offsets)
    got = exchanged(packed, ("pitch", "inst"))
    sent = pl.pallas_call(
        functools.partial(transfer_kernel, inst_dev, blocks, members),
        out_shape=jax.ShapeDtypeStruct((peers * depth, lanes), jnp.float32),
        in_specs=[VMEM, VMEM, VMEM],
        out_specs=VMEM,
        scratch_shapes=[
            pltpu.VMEM((used * (2 * blocks + 1), lanes), jnp.float32),
            pltpu.SMEM((2 * count * members,), jnp.int32),
            pltpu.SemaphoreType.DMA(()),
        ],
        compiler_params=params(24),
    )(got, mix, starts)
    back = exchanged(sent, ("inst", "pitch"))
    return pl.pallas_call(
        functools.partial(unpack_kernel, blocks, owners),
        out_shape=jax.ShapeDtypeStruct(donor_state.shape, jnp.float32),
        in_specs=[VMEM],
        out_specs=hbm,
        scratch_shapes=[pltpu.VMEM(donor_state.shape, jnp.float32), pltpu.SemaphoreType.DMA((2, inst_dev))],
        compiler_params=params(8),
    )(back)


def solution(mesh):
    return jax.shard_map(
        on_device,
        mesh=mesh,
        in_specs=(P(None, "inst", None, "span", "pitch"), P(), P(), P(None, None, "pitch"), P()),
        out_specs=P(None, "inst", None, "span", "pitch"),
        check_vma=False,
    )
```
